512 devices in a mesh: front: 8 (over x, y_hi), row: 8 (over z), col: 8 (over y_lo, core).
Axes of the slice: x: 4, y: 8 (y_hi: 2, y_lo: 4; y = y_hi * 4 + y_lo), z: 8, core: 2. Of those that a mesh axis runs over, the one named last changes fastest.
Arguments:
- parent_front: bfloat16 [8, 8192, 4096], P('front', 'row', 'col'), may hold values from -3 to 28, as said below
- child_front: bfloat16 [8, 4096, 4096], P('front', 'row', 'col'), may hold values from -2 to 2, as said below
- child_blocks: int32 [8, 16], replicated, may hold values from 0 to 31, as said below
- child_mask: int32 [8, 16, 16], replicated, may hold values from 0 to 1, as said below
Outputs:
- factored_front: float32 [8, 8192, 4096], P('front', 'row', 'col')
The draws below stay inside these ranges and needn't reach their ends.
Inputs may be any that keep to these rules, and one draw needn't show every extreme that they name: `parent_front`: each parent's matrix is symmetric, and its sum with the extend-add of its two children's masked contributions is positive definite. `child_front`: each child's contribution is symmetric. `child_blocks`: for child c, the tiles a with a % 8 == r map to distinct parent tiles congruent to r modulo 8 that rise with a, and one of them is the last such parent tile. `child_mask`: symmetric in its last two dimensions, with ones on the diagonal.
All inputs are finite; a program needn't handle non-finite values.
Results may differ from the reference program's by a relative error of at most 0.0003.
Values may be sent and summed in bfloat16 or wider, within the bound.
No kernel may reach another device: no remote copies, remote signals or barrier semaphores. Data moves between devices by JAX's collectives and lax.ppermute only.
A program may use at most 64 MiB of HBM per device.

```python
import math
import jax
import jax.numpy as jnp
from jax import lax

WP = 8192
WC = 4096
B = 256
PANELS = 2
GROUPS = 8
GRID_ROWS = 8
GRID_COLS = 8
N_FRONT = 8
N_ROW = 8
N_COL = 8


def symmetric_field(key, width, scale):
    raw_values = jnp.clip(jax.random.normal(key, (width, width), jnp.float32), -6.0, 6.0)
    return (raw_values + raw_values.T) * (scale * 0.70710678)


def coupling_vector(key, width):
    spread = 3.0 / math.sqrt(B)
    factors = jnp.clip(jax.random.normal(key, (width,), jnp.float32), -4.0, 4.0)
    return factors * spread


def parent_storage(dense):
    row_slots = WP // (B * GRID_ROWS)
    col_slots = WP // (B * 2 * GRID_COLS)
    row_order = dense.reshape(row_slots, GRID_ROWS, B, WP).transpose(1, 0, 2, 3).reshape(WP, WP)
    arranged = row_order.reshape(WP, col_slots, 2, GRID_COLS, B).transpose(2, 0, 3, 1, 4)
    odd_cols = (jnp.arange(GRID_COLS) % 2 == 1)[None, None, :, None, None]
    arranged = jnp.where(odd_cols, arranged[::-1], arranged)
    return arranged.reshape(2, WP, WP // 2)


def child_storage(dense):
    row_slots = WC // (B * GRID_ROWS)
    col_slots = WC // (B * GRID_COLS)
    row_order = dense.reshape(row_slots, GRID_ROWS, B, WC).transpose(1, 0, 2, 3).reshape(WC, WC)
    return row_order.reshape(WC, col_slots, GRID_COLS, B).transpose(0, 2, 1, 3).reshape(WC, WC)


def draw_parent_front(key, part):
    pieces = []
    positions = jnp.arange(WP)
    for parent in range(GROUPS // 2):
        parent_key = jax.random.fold_in(key, parent)
        field = symmetric_field(jax.random.fold_in(parent_key, 1), WP, 1.5 / math.sqrt(WP))
        diagonal = jax.random.uniform(jax.random.fold_in(parent_key, 2), (WP,), jnp.float32, 12.0, 24.0)
        field = jnp.where(positions[:, None] == positions[None, :], diagonal[:, None], field)
        for term in range(2):
            vector = coupling_vector(jax.random.fold_in(parent_key, 10 + term), WP)
            field = field + vector[:, None] * vector[None, :]
        pieces.append(parent_storage(field))
    return jnp.concatenate(pieces, axis=0).astype(jnp.bfloat16)


def draw_child_front(key, part):
    pieces = []
    for child_index in range(GROUPS):
        field = symmetric_field(jax.random.fold_in(key, child_index), WC, 1.5 / math.sqrt(WC))
        pieces.append(child_storage(field)[None])
    return jnp.concatenate(pieces, axis=0).astype(jnp.bfloat16)


def draw_child_blocks(key, part):
    row_slots = WP // (B * GRID_ROWS)
    child_slots = WC // (B * GRID_ROWS)
    keys = jax.random.split(key, GROUPS * GRID_ROWS)

    def choose_slots(one_key):
        order = jax.random.permutation(one_key, row_slots - 1)[:child_slots - 1]
        joined = jnp.concatenate([order.astype(jnp.int32), jnp.full((1,), row_slots - 1, jnp.int32)])
        return jnp.sort(joined)
    chosen = jax.vmap(choose_slots)(keys).reshape(GROUPS, GRID_ROWS, child_slots)
    residue = jnp.arange(GRID_ROWS, dtype=jnp.int32)[None, :, None]
    blocks = residue + GRID_ROWS * chosen
    return blocks.transpose(0, 2, 1).reshape(GROUPS, child_slots * GRID_ROWS).astype(jnp.int32)


def draw_child_mask(key, part):
    tile_count = WC // B
    upper = (jax.random.randint(key, (GROUPS, tile_count, tile_count), 0, 4) > 0).astype(jnp.int32)
    row_ids = jnp.arange(tile_count)[:, None]
    col_ids = jnp.arange(tile_count)[None, :]
    mirrored = jnp.where(row_ids < col_ids, upper, jnp.swapaxes(upper, 1, 2))
    return jnp.where(row_ids == col_ids, 1, mirrored).astype(jnp.int32)


def setup_inputs(seed: int = 0) -> dict:
    seeds = jax.random.split(jax.random.key(seed), 5)
    return {
        "parent_front": draw_parent_front(jax.random.fold_in(seeds[4], 71), 0),
        "child_front": draw_child_front(jax.random.fold_in(seeds[4], 71), 0),
        "child_blocks": draw_child_blocks(jax.random.fold_in(seeds[4], 71), 0),
        "child_mask": draw_child_mask(jax.random.fold_in(seeds[4], 71), 0),
    }


def swap_halves(arranged):
    odd_cols = (jnp.arange(N_COL) % 2 == 1)[None, None, :, None, None]
    return jnp.where(odd_cols, arranged[::-1], arranged)

def parent_dense(stored):
    row_slots = WP // (B * N_ROW)
    col_slots = WP // (B * 2 * N_COL)
    arranged = swap_halves(stored.reshape(2, WP, N_COL, col_slots, B))
    col_order = arranged.transpose(1, 3, 0, 2, 4).reshape(WP, WP)
    return col_order.reshape(N_ROW, row_slots, B, WP).transpose(1, 0, 2, 3).reshape(WP, WP)

def parent_stored(dense):
    row_slots = WP // (B * N_ROW)
    col_slots = WP // (B * 2 * N_COL)
    row_order = dense.reshape(row_slots, N_ROW, B, WP).transpose(1, 0, 2, 3).reshape(WP, WP)
    arranged = row_order.reshape(WP, col_slots, 2, N_COL, B).transpose(2, 0, 3, 1, 4)
    return swap_halves(arranged).reshape(2, WP, WP // 2)

def child_dense(stored):
    row_slots = WC // (B * N_ROW)
    col_slots = WC // (B * N_COL)
    col_order = stored.reshape(WC, N_COL, col_slots, B).transpose(0, 2, 1, 3).reshape(WC, WC)
    return col_order.reshape(N_ROW, row_slots, B, WC).transpose(1, 0, 2, 3).reshape(WC, WC)

def scatter_child(front_matrix, stored, block_map, tile_mask):
    tile_count = WC // B
    update = child_dense(stored.astype(jnp.float32))
    update = (update.reshape(tile_count, B, tile_count, B) * tile_mask.astype(jnp.float32)[:, None, :, None]).reshape(WC, WC)
    scatter_index = (block_map[:, None] * B + jnp.arange(B, dtype=jnp.int32)[None, :]).reshape(WC).astype(jnp.int32)
    return front_matrix.at[scatter_index[:, None], scatter_index[None, :]].add(update)

def factor_panels(front_matrix):
    for panel_step in range(PANELS):
        first_col = panel_step * B
        after_col = first_col + B
        pivot_factor = jnp.linalg.cholesky(front_matrix[first_col:after_col, first_col:after_col])
        panel_below = lax.linalg.triangular_solve(pivot_factor, front_matrix[after_col:, first_col:after_col], left_side=False, lower=True, transpose_a=True)
        product = jnp.dot(panel_below.astype(jnp.float32), panel_below.T.astype(jnp.float32), precision=lax.Precision.HIGHEST, preferred_element_type=jnp.float32)
        front_matrix = front_matrix.at[after_col:, after_col:].add(-product)
        front_matrix = front_matrix.at[first_col:after_col, first_col:].set(0.0)
        front_matrix = front_matrix.at[first_col:after_col, first_col:after_col].set(pivot_factor)
        front_matrix = front_matrix.at[after_col:, first_col:after_col].set(panel_below)
    return front_matrix

def reference(parent_front, child_front, child_blocks, child_mask):
    outputs = []
    for parent in range(N_FRONT // 2):
        front_matrix = parent_dense(parent_front[2 * parent:2 * parent + 2].astype(jnp.float32))
        for child_index in (2 * parent, 2 * parent + 1):
            front_matrix = scatter_child(front_matrix, child_front[child_index], child_blocks[child_index], child_mask[child_index])
        outputs.append(parent_stored(factor_panels(front_matrix)))
    return jnp.concatenate(outputs, axis=0)
```

```python
import jax
import jax.numpy as jnp
from jax import lax
from jax.experimental import pallas as pl
from jax.experimental.pallas import tpu as pltpu
from jax.sharding import Mesh
from jax.sharding import PartitionSpec as P

B = 256
H = 128
F32 = jnp.float32
BF16 = jnp.bfloat16


def matmul(a, b, dims, precision=lax.Precision.HIGHEST):
    return lax.dot_general(a, b, (dims, ((), ())), precision=precision, preferred_element_type=F32)


NT = ((1,), (1,))
NN = ((1,), (0,))


def split(a):
    high = a.astype(BF16)
    return high, (a - high.astype(F32)).astype(BF16)


def three_pass(a, b, dims):
    (ah, al), (bh, bl) = a, b
    dot = lambda x, y: lax.dot_general(x, y, (dims, ((), ())), preferred_element_type=F32)
    return dot(ah, bh) + (dot(ah, bl) + dot(al, bh))


def inverse_factor(strips):
    sub = lax.broadcasted_iota(jnp.int32, (8, H), 0)
    lane = lax.broadcasted_iota(jnp.int32, (8, H), 1)
    count = H // 8
    body = list(strips)
    inv = [(lane == sub + 8 * s).astype(F32) for s in range(count)]
    row_of = lambda v, j: jnp.broadcast_to(v[j : j + 1, :], (8, H))
    for s in range(count):
        cols = {
            t: [jnp.broadcast_to(body[t][:, 8 * s + j : 8 * s + j + 1], (8, H)) for j in range(8)]
            for t in range(s, count)
        }
        for j in range(8):
            scale = lax.rsqrt(row_of(cols[s][j], j))
            row_body = row_of(body[s], j) * scale
            row_inv = row_of(inv[s], j) * scale
            own = cols[s][j] * scale
            coeff = {m: row_of(own, m) for m in range(j + 1, 8)}
            for t in range(s, count):
                col = own if t == s else cols[t][j] * scale
                for m in range(j + 1, 8):
                    cols[t][m] = cols[t][m] - col * coeff[m]
                if t == s:
                    low = jnp.where(sub > j, col, 0.0)
                    body[t] = body[t] - low * row_body
                    inv[t] = jnp.where(sub == j, row_inv, inv[t] - low * row_inv)
                else:
                    body[t] = body[t] - col * row_body
                    inv[t] = inv[t] - col * row_inv
    return jnp.concatenate(inv, axis=0)


def at(k):
    return slice(k * H, (k + 1) * H)


def factor_tile(work, first):
    inv, low = {}, {}
    last = first + 1
    for b in (first, last):
        inv[b] = inverse_factor(
            [work[b * H + 8 * s : b * H + 8 * s + 8, at(b)] for s in range(H // 8)]
        )
        if b == first:
            low = matmul(work[at(last), at(b)], inv[b], NT)
            work[at(last), at(last)] -= matmul(low, low, NT)
    return inv[first], inv[last], -matmul(inv[last], matmul(low, inv[first], NN), NN)


def store_inverse(x_ref, blocks):
    top, low, corner = blocks
    x_ref[0:H, 0:H] = top
    x_ref[H:, H:] = low
    x_ref[0:H, H:] = jnp.zeros((H, H), F32)
    x_ref[H:, 0:H] = corner


def first_kernel(where, mine_ref, theirs_ref, x0_ref, l10_ref, rest_ref, work):
    even = where[2] == 0
    work[...] = jnp.where(even, mine_ref[0:B], theirs_ref[0:B])
    store_inverse(x0_ref, factor_tile(work, 0))
    d01 = jnp.where(even, theirs_ref[0:B], mine_ref[0:B])
    low = matmul(d01.T, x0_ref[...], NT)
    l10_ref[...] = low
    rest_ref[...] = jnp.where(even, theirs_ref[B:], mine_ref[B:]) - matmul(low, low, NT)


def second_kernel(rest_ref, x1_ref, work):
    work[...] = rest_ref[...]
    store_inverse(x1_ref, factor_tile(work, 0))


TILE = jax.ShapeDtypeStruct((B, B), F32)
VMEM = pl.BlockSpec(memory_space=pltpu.VMEM)
COST = pl.CostEstimate(flops=10**10, bytes_accessed=2**20, transcendentals=0)
PARAMS = pltpu.CompilerParams(vmem_limit_bytes=32 * 2**20)


def first_pivot(where, mine, theirs):
    return pl.pallas_call(
        first_kernel,
        out_shape=(TILE, TILE, TILE),
        in_specs=[pl.BlockSpec(memory_space=pltpu.SMEM), VMEM, VMEM],
        scratch_shapes=[pltpu.VMEM((B, B), F32)],
        compiler_params=PARAMS,
        cost_estimate=COST,
    )(where, mine, theirs)


def second_pivot(rest):
    return pl.pallas_call(
        second_kernel,
        out_shape=TILE,
        in_specs=[VMEM],
        scratch_shapes=[pltpu.VMEM((B, B), F32)],
        compiler_params=PARAMS,
        cost_estimate=COST,
    )(rest)


def final_kernel(
    place, where, parent_ref, own_ref, top_ref, low_ref, mine_ref, theirs_ref, g_ref, h_ref,
    x0_ref, x1_ref, l10_ref, out_ref, across, xs,
):
    slot = pl.program_id(0)

    @pl.when(slot == 0)
    def _():
        for k, ref in enumerate((x0_ref, x1_ref, l10_ref)):
            xs[2 * k], xs[2 * k + 1] = split(ref[...])
        x0, x1, l10 = [(xs[2 * k], xs[2 * k + 1]) for k in range(3)]
        dot = lambda a, b: lax.dot_general(a, b, (NN, ((), ())), preferred_element_type=F32)
        g = g_ref[...]
        q0 = dot(x0[0], g) + dot(x0[1], g)
        q1 = three_pass(x1, split(h_ref[...].astype(F32) - three_pass(l10, split(q0), NN)), NN)
        across[0:B] = q0.astype(BF16)
        across[B:] = q1.astype(BF16)

    x0, x1, l10 = [(xs[2 * k], xs[2 * k + 1]) for k in range(3)]
    even = where[2] == 0
    mine, theirs = mine_ref[...], theirs_ref[...]
    p0 = three_pass(split(jnp.where(even, mine, theirs)), x0, NT)
    p0s = split(p0)
    p1 = three_pass(split(jnp.where(even, theirs, mine) - three_pass(p0s, l10, NT)), x1, NT)
    p1s = split(p1)
    row = where[0] + 8 * slot
    lead = row < 2
    last = (slot == 3).astype(jnp.int32)
    from_row = pl.multiple_of(last * B, B)
    for v in range(2):
        cols = slice(v * B, (v + 1) * B)
        value = parent_ref[:, cols].astype(F32)
        for b in range(v + 1):
            here = slice(b * B, (b + 1) * B)
            sib = jnp.where(last == 1, low_ref[:, here].astype(F32), top_ref[:, here].astype(F32))
            own = own_ref[pl.ds(from_row, B), here].astype(F32)
            for child, part in enumerate((own, sib)):
                w = place[(((child * 2 + last) * 2 + b) * 4 + slot) * 2 + v]
                value += w * part
        q0, q1 = across[0:B, cols], across[B:, cols]
        dot = lambda a, b: lax.dot_general(a, b, (NN, ((), ())), preferred_element_type=F32)
        value -= (dot(p0s[0], q0) + dot(p1s[0], q1)) + (dot(p0s[1], q0) + dot(p1s[1], q1))
        out_ref[:, cols] = jnp.where(lead, 0.0, value)
    tril = lax.broadcasted_iota(jnp.int32, (B, B), 0) >= lax.broadcasted_iota(jnp.int32, (B, B), 1)

    @pl.when(where[1] == 0)
    def _():
        out_ref[:, 0:B] = jnp.where(jnp.logical_or(tril, row > 0), p0, 0.0)

    @pl.when(where[1] == 1)
    def _():
        keep = jnp.logical_and(jnp.logical_or(tril, row > 1), row > 0)
        out_ref[:, 0:B] = jnp.where(keep, p1, 0.0)


def finish(place, where, parent, own, top, low, mine, theirs, g, h, x0, x1, l10):
    whole = lambda shape: pl.BlockSpec(shape, lambda i, *_: (0, 0))
    rows = lambda width: pl.BlockSpec((B, width), lambda i, *_: (i, 0))
    wide, tile = whole((B, 2 * B)), whole((B, B))
    return pl.pallas_call(
        final_kernel,
        out_shape=jax.ShapeDtypeStruct(parent.shape, F32),
        grid_spec=pltpu.PrefetchScalarGridSpec(
            num_scalar_prefetch=2,
            grid=(parent.shape[0] // B,),
            in_specs=[
                rows(2 * B), whole((2 * B, 2 * B)), wide, wide, rows(B), rows(B),
                wide, wide, tile, tile, tile,
            ],
            out_specs=rows(2 * B),
            scratch_shapes=[pltpu.VMEM((2 * B, 2 * B), BF16), pltpu.VMEM((6, B, B), BF16)],
        ),
        compiler_params=pltpu.CompilerParams(vmem_limit_bytes=48 * 2**20),
    )(place, where, parent, own, top, low, mine, theirs, g, h, x0, x1, l10)


def tie(value, *after):
    return lax.optimization_barrier((value, *after))[0]


def one_of(index, places):
    hit = index == places[0]
    for place in places[1:]:
        hit = jnp.logical_or(hit, index == place)
    return hit


class Along:
    def __init__(self, axes, index, first, second, third, fourth, zero, one):
        self.axes, self.index = axes, index
        self.routes = first, second, third, fourth
        self.zero, self.one = zero, one

    def send(self, value, k):
        return lax.ppermute(value, self.axes, self.routes[k])

    def start(self, block):
        first, second = self.send(block, 0), self.send(block, 1)
        ends = lambda k: [dst for _, dst in self.routes[k]]
        return jnp.where(
            one_of(self.index, ends(0)), first, jnp.where(one_of(self.index, ends(1)), second, block)
        )

    def end(self, held):
        third, fourth = self.send(held, 2), self.send(held, 3)
        pick = lambda own, near: jnp.where(
            one_of(self.index, own), held, jnp.where(one_of(self.index, near), third, fourth)
        )
        return pick(*self.zero), pick(*self.one)


def ring_y(y):
    return Along(
        ("y_hi", "y_lo"), y, [(0, 3), (4, 7)], [(0, 5), (4, 1)],
        [(0, 1), (3, 4), (5, 6), (4, 5), (7, 0), (1, 2)], [(0, 7), (3, 2), (4, 3), (7, 6)],
        ((0, 3, 5), (1, 4, 6)), ((4, 7, 1), (5, 0, 2)),
    )


def ring_z(z):
    return Along(
        "row", z, [(0, 5), (1, 4)], [(0, 2), (1, 7)],
        [(0, 1), (5, 4), (2, 3), (1, 2), (4, 5), (7, 6)], [(0, 7), (5, 6), (1, 0), (4, 3)],
        ((0, 2, 5), (1, 3, 4)), ((1, 4, 7), (2, 5, 6)),
    )


def direct_z(block, z, before_last):
    late = tie(block, before_last)
    recv = [
        lax.ppermute(
            block if s < 5 else late, ("row", "core"), [(0, 2 * s), (1, 2 * s + 1), (3, 2 * ((1 + s) % 8) + 1)]
        )
        for s in range(1, 8)
    ]
    zero, one = block, block
    for s in range(1, 8):
        zero = jnp.where(z == s, recv[s - 1], zero)
        one = jnp.where(z == (1 + s) % 8, recv[s - 1], one)
    return jnp.concatenate([zero, one], axis=0), recv[0]


def on_device(parent, child, child_blocks, child_mask):
    parent, child = parent[0], child[0]
    x, half = lax.axis_index("x"), lax.axis_index("y_hi")
    z, y_lo, core = lax.axis_index("row"), lax.axis_index("y_lo"), lax.axis_index("core")
    z = z.astype(jnp.int32)
    y = half * 4 + y_lo
    col = 2 * y_lo + core
    other = lambda value: lax.ppermute(value, "core", [(0, 1), (1, 0)])

    maps = lax.dynamic_slice(child_blocks, (2 * x, 0), (2, 16))
    masks = lax.dynamic_slice(child_mask, (2 * x, 0, 0), (2, 16, 16))
    down = lax.dynamic_index_in_dim(maps.reshape(2, 2, 8), z, 2, keepdims=False)
    over = lax.dynamic_index_in_dim(maps.reshape(2, 2, 8), col, 2, keepdims=False)
    mask_rows = lax.dynamic_index_in_dim(masks.reshape(2, 2, 8, 16), z, 2, keepdims=False)
    mask_here = lax.dynamic_index_in_dim(mask_rows.reshape(2, 2, 2, 8), col, 3, keepdims=False)
    mask_core = lax.dynamic_index_in_dim(mask_rows, core, 2, keepdims=False)
    first_col = (half + y_lo * 2 + core) % 2 * 8 + col
    row_hit = down[:, :, None] == 8 * jnp.arange(4) + z
    col_hit = over[:, :, None] == 16 * jnp.arange(2) + first_col
    place = (
        row_hit[:, :, None, :, None]
        & col_hit[:, None, :, None, :]
        & (mask_here > 0)[:, :, :, None, None]
    ).astype(F32)
    panel_hit = lax.dynamic_index_in_dim(maps, core, 1, keepdims=False) == core
    panel_place = (row_hit & (mask_core > 0)[:, :, None] & panel_hit[:, None, None]).astype(F32)

    place = jnp.where(half == 1, place[::-1], place)
    special = jnp.where(
        jnp.logical_and(half == 0, col == 0), 0, jnp.where(jnp.logical_and(half == 1, col == 1), 1, 2)
    )
    where = jnp.stack([z, special, core]).astype(jnp.int32)
    spread_y, spread_z = ring_y(y), ring_z(z)
    swap = lambda value: lax.ppermute(value, "y_hi", [(0, 1), (1, 0)])

    lead = jnp.concatenate([parent[:B, :B], child[:B, :B]], axis=0)
    held = spread_y.start(lead)
    from0, from4 = spread_y.end(held)
    base = jnp.where(core == 0, from0[:B], from4[:B]).astype(F32)
    childs = [from0[B:].astype(F32), from4[B:].astype(F32)]
    top = base + panel_place[0, 0, 0] * childs[0] + panel_place[1, 0, 0] * childs[1]
    sib_top = swap(tie(child[:B], held))
    pivot_rows, early = direct_z(top, z, sib_top)
    theirs = other(pivot_rows)

    rest = jnp.concatenate([parent[B:, :B], child[B:, :B]], axis=0)
    rest_held = spread_y.start(tie(rest, early))

    strip = parent[:B].astype(F32).reshape(B, 2, B)
    for k, ref in ((0, child[:B]), (1, sib_top)):
        for b in range(2):
            strip += place[k, 0, b, 0][None, :, None] * ref[:, None, b * B : (b + 1) * B].astype(F32)
    strip_held = spread_z.start(tie(strip.reshape(B, 2 * B).astype(BF16), early))
    rest0, rest4 = spread_y.end(tie(rest_held, pivot_rows))

    x0, l10, low = first_pivot(tie(where, strip_held), pivot_rows, theirs)
    g, h = spread_z.end(tie(strip_held, pivot_rows))
    sib_low = swap(tie(child[B:], rest_held))
    tiles = jnp.where(core == 0, rest0[: 3 * B], rest4[: 3 * B]).astype(F32)
    below = [
        tiles[(s - 1) * B : s * B]
        + panel_place[0, s // 3, s] * (rest0[3 * B :].astype(F32) if s == 3 else childs[0])
        + panel_place[1, s // 3, s] * (rest4[3 * B :].astype(F32) if s == 3 else childs[1])
        for s in range(1, 4)
    ]
    column = jnp.concatenate([top, *below], axis=0)
    column_other = other(tie(column, x0))
    x1 = second_pivot(tie(low, column))
    out = finish(
        place.reshape(-1), where, parent, child, sib_top, sib_low, column, column_other,
        g, h, x0, x1, l10,
    )
    return out[None]


def solution(mesh):
    shape = mesh.shape
    if (shape["front"], shape["row"], shape["col"]) != (8, 8, 8):
        raise ValueError("mesh shape")
    fine = Mesh(
        mesh.devices.reshape(4, 2, 8, 4, 2), ("x", "y_hi", "row", "y_lo", "core")
    )
    spec = P(("x", "y_hi"), "row", ("y_lo", "core"))
    return jax.shard_map(
        on_device, mesh=fine, in_specs=(spec, spec, P(), P()), out_specs=spec, check_vma=False
    )
```

```python
import jax
import jax.numpy as jnp
from jax import lax
from jax.experimental import pallas as pl
from jax.experimental.pallas import tpu as pltpu
from jax.sharding import Mesh
from jax.sharding import PartitionSpec as P

B = 256
H = 128
F32 = jnp.float32
BF16 = jnp.bfloat16


def matmul(a, b, dims, precision=lax.Precision.HIGHEST):
    return lax.dot_general(a, b, (dims, ((), ())), precision=precision, preferred_element_type=F32)


NT = ((1,), (1,))
NN = ((1,), (0,))


def split(a):
    high = a.astype(BF16)
    return high, (a - high.astype(F32)).astype(BF16)


def three_pass(a, b, dims):
    (ah, al), (bh, bl) = a, b
    dot = lambda x, y: lax.dot_general(x, y, (dims, ((), ())), preferred_element_type=F32)
    return dot(ah, bh) + (dot(ah, bl) + dot(al, bh))


def inverse_factor(strips):
    sub = lax.broadcasted_iota(jnp.int32, (8, H), 0)
    lane = lax.broadcasted_iota(jnp.int32, (8, H), 1)
    count = H // 8
    body = list(strips)
    inv = [(lane == sub + 8 * s).astype(F32) for s in range(count)]
    row_of = lambda v, j: jnp.broadcast_to(v[j : j + 1, :], (8, H))
    for s in range(count):
        cols = {
            t: [jnp.broadcast_to(body[t][:, 8 * s + j : 8 * s + j + 1], (8, H)) for j in range(8)]
            for t in range(s, count)
        }
        for j in range(8):
            scale = lax.rsqrt(row_of(cols[s][j], j))
            row_body = row_of(body[s], j) * scale
            row_inv = row_of(inv[s], j) * scale
            own = cols[s][j] * scale
            coeff = {m: row_of(own, m) for m in range(j + 1, 8)}
            for t in range(s, count):
                col = own if t == s else cols[t][j] * scale
                for m in range(j + 1, 8):
                    cols[t][m] = cols[t][m] - col * coeff[m]
                if t == s:
                    low = jnp.where(sub > j, col, 0.0)
                    body[t] = body[t] - low * row_body
                    inv[t] = jnp.where(sub == j, row_inv, inv[t] - low * row_inv)
                else:
                    body[t] = body[t] - col * row_body
                    inv[t] = inv[t] - col * row_inv
    return jnp.concatenate(inv, axis=0)


def at(k):
    return slice(k * H, (k + 1) * H)


def factor_tile(work, first):
    inv, low = {}, {}
    last = first + 1
    for b in (first, last):
        inv[b] = inverse_factor(
            [work[b * H + 8 * s : b * H + 8 * s + 8, at(b)] for s in range(H // 8)]
        )
        if b == first:
            low = matmul(work[at(last), at(b)], inv[b], NT)
            work[at(last), at(last)] -= matmul(low, low, NT)
    return inv[first], inv[last], -matmul(inv[last], matmul(low, inv[first], NN), NN)


def store_inverse(x_ref, blocks):
    top, low, corner = blocks
    x_ref[0:H, 0:H] = top
    x_ref[H:, H:] = low
    x_ref[0:H, H:] = jnp.zeros((H, H), F32)
    x_ref[H:, 0:H] = corner


def first_kernel(where, mine_ref, theirs_ref, x0_ref, l10_ref, rest_ref, work):
    even = where[2] == 0
    work[...] = jnp.where(even, mine_ref[0:B], theirs_ref[0:B])
    store_inverse(x0_ref, factor_tile(work, 0))
    d01 = jnp.where(even, theirs_ref[0:B], mine_ref[0:B])
    low = matmul(d01.T, x0_ref[...], NT)
    l10_ref[...] = low
    rest_ref[...] = jnp.where(even, theirs_ref[B:], mine_ref[B:]) - matmul(low, low, NT)


def second_kernel(rest_ref, x1_ref, work):
    work[...] = rest_ref[...]
    store_inverse(x1_ref, factor_tile(work, 0))


TILE = jax.ShapeDtypeStruct((B, B), F32)
VMEM = pl.BlockSpec(memory_space=pltpu.VMEM)
COST = pl.CostEstimate(flops=10**10, bytes_accessed=2**20, transcendentals=0)
PARAMS = pltpu.CompilerParams(vmem_limit_bytes=32 * 2**20)


def first_pivot(where, mine, theirs):
    return pl.pallas_call(
        first_kernel,
        out_shape=(TILE, TILE, TILE),
        in_specs=[pl.BlockSpec(memory_space=pltpu.SMEM), VMEM, VMEM],
        scratch_shapes=[pltpu.VMEM((B, B), F32)],
        compiler_params=PARAMS,
        cost_estimate=COST,
    )(where, mine, theirs)


def second_pivot(rest):
    return pl.pallas_call(
        second_kernel,
        out_shape=TILE,
        in_specs=[VMEM],
        scratch_shapes=[pltpu.VMEM((B, B), F32)],
        compiler_params=PARAMS,
        cost_estimate=COST,
    )(rest)


def final_kernel(
    place, where, parent_ref, own_ref, sib_ref, mine_ref, theirs_ref, g_ref, h_ref,
    x0_ref, x1_ref, l10_ref, out_ref, across, xs,
):
    slot = pl.program_id(0)

    @pl.when(slot == 0)
    def _():
        for k, ref in enumerate((x0_ref, x1_ref, l10_ref)):
            xs[2 * k], xs[2 * k + 1] = split(ref[...])
        x0, x1, l10 = [(xs[2 * k], xs[2 * k + 1]) for k in range(3)]
        dot = lambda a, b: lax.dot_general(a, b, (NN, ((), ())), preferred_element_type=F32)
        g = g_ref[...]
        q0 = dot(x0[0], g) + dot(x0[1], g)
        q1 = three_pass(x1, split(h_ref[...].astype(F32) - three_pass(l10, split(q0), NN)), NN)
        across[0:B] = q0.astype(BF16)
        across[B:] = q1.astype(BF16)

    x0, x1, l10 = [(xs[2 * k], xs[2 * k + 1]) for k in range(3)]
    even = where[2] == 0
    mine, theirs = mine_ref[...], theirs_ref[...]
    p0 = three_pass(split(jnp.where(even, mine, theirs)), x0, NT)
    p0s = split(p0)
    p1 = three_pass(split(jnp.where(even, theirs, mine) - three_pass(p0s, l10, NT)), x1, NT)
    p1s = split(p1)
    row = where[0] + 8 * slot
    lead = row < 2
    last = (slot == 3).astype(jnp.int32)
    from_row = pl.multiple_of(last * B, B)
    for v in range(2):
        cols = slice(v * B, (v + 1) * B)
        value = parent_ref[:, cols].astype(F32)
        for b in range(v + 1):
            here = slice(b * B, (b + 1) * B)
            for child, ref in enumerate((own_ref, sib_ref)):
                part = ref[pl.ds(from_row, B), here].astype(F32)
                w = place[(((child * 2 + last) * 2 + b) * 4 + slot) * 2 + v]
                value += w * part
        q0, q1 = across[0:B, cols], across[B:, cols]
        dot = lambda a, b: lax.dot_general(a, b, (NN, ((), ())), preferred_element_type=F32)
        value -= (dot(p0s[0], q0) + dot(p1s[0], q1)) + (dot(p0s[1], q0) + dot(p1s[1], q1))
        out_ref[:, cols] = jnp.where(lead, 0.0, value)
    tril = lax.broadcasted_iota(jnp.int32, (B, B), 0) >= lax.broadcasted_iota(jnp.int32, (B, B), 1)

    @pl.when(where[1] == 0)
    def _():
        out_ref[:, 0:B] = jnp.where(jnp.logical_or(tril, row > 0), p0, 0.0)

    @pl.when(where[1] == 1)
    def _():
        keep = jnp.logical_and(jnp.logical_or(tril, row > 1), row > 0)
        out_ref[:, 0:B] = jnp.where(keep, p1, 0.0)


def finish(place, where, parent, own, sib, mine, theirs, g, h, x0, x1, l10):
    whole = lambda shape: pl.BlockSpec(shape, lambda i, *_: (0, 0))
    rows = lambda width: pl.BlockSpec((B, width), lambda i, *_: (i, 0))
    wide, tile = whole((B, 2 * B)), whole((B, B))
    return pl.pallas_call(
        final_kernel,
        out_shape=jax.ShapeDtypeStruct(parent.shape, F32),
        grid_spec=pltpu.PrefetchScalarGridSpec(
            num_scalar_prefetch=2,
            grid=(parent.shape[0] // B,),
            in_specs=[
                rows(2 * B), whole((2 * B, 2 * B)), whole((2 * B, 2 * B)), rows(B), rows(B),
                wide, wide, tile, tile, tile,
            ],
            out_specs=rows(2 * B),
            scratch_shapes=[pltpu.VMEM((2 * B, 2 * B), BF16), pltpu.VMEM((6, B, B), BF16)],
        ),
        compiler_params=pltpu.CompilerParams(vmem_limit_bytes=48 * 2**20),
    )(place, where, parent, own, sib, mine, theirs, g, h, x0, x1, l10)


def tie(value, *after):
    return lax.optimization_barrier((value, *after))[0]


def one_of(index, places):
    hit = index == places[0]
    for place in places[1:]:
        hit = jnp.logical_or(hit, index == place)
    return hit


class Along:
    def __init__(self, axes, index, first, second, third, fourth, zero, one):
        self.axes, self.index = axes, index
        self.routes = first, second, third, fourth
        self.zero, self.one = zero, one

    def send(self, value, k):
        return lax.ppermute(value, self.axes, self.routes[k])

    def start(self, block):
        first, second = self.send(block, 0), self.send(block, 1)
        ends = lambda k: [dst for _, dst in self.routes[k]]
        return jnp.where(
            one_of(self.index, ends(0)), first, jnp.where(one_of(self.index, ends(1)), second, block)
        )

    def end(self, held):
        third, fourth = self.send(held, 2), self.send(held, 3)
        pick = lambda own, near: jnp.where(
            one_of(self.index, own), held, jnp.where(one_of(self.index, near), third, fourth)
        )
        return pick(*self.zero), pick(*self.one)


def ring_y(y):
    return Along(
        ("y_hi", "y_lo"), y, [(0, 3), (4, 7)], [(0, 5), (4, 1)],
        [(0, 1), (3, 4), (5, 6), (4, 5), (7, 0), (1, 2)], [(0, 7), (3, 2), (4, 3), (7, 6)],
        ((0, 3, 5), (1, 4, 6)), ((4, 7, 1), (5, 0, 2)),
    )


def ring_z(z):
    return Along(
        "row", z, [(0, 5), (1, 4)], [(0, 2), (1, 7)],
        [(0, 1), (5, 4), (2, 3), (1, 2), (4, 5), (7, 6)], [(0, 7), (5, 6), (1, 0), (4, 3)],
        ((0, 2, 5), (1, 3, 4)), ((1, 4, 7), (2, 5, 6)),
    )


def on_device(parent, child, child_blocks, child_mask):
    parent, child = parent[0], child[0]
    x, half = lax.axis_index("x"), lax.axis_index("y_hi")
    z, y_lo, core = lax.axis_index("row"), lax.axis_index("y_lo"), lax.axis_index("core")
    z = z.astype(jnp.int32)
    y = half * 4 + y_lo
    col = 2 * y_lo + core
    other = lambda value: lax.ppermute(value, "core", [(0, 1), (1, 0)])

    maps = lax.dynamic_slice(child_blocks, (2 * x, 0), (2, 16))
    masks = lax.dynamic_slice(child_mask, (2 * x, 0, 0), (2, 16, 16))
    down = lax.dynamic_index_in_dim(maps.reshape(2, 2, 8), z, 2, keepdims=False)
    over = lax.dynamic_index_in_dim(maps.reshape(2, 2, 8), col, 2, keepdims=False)
    mask_rows = lax.dynamic_index_in_dim(masks.reshape(2, 2, 8, 16), z, 2, keepdims=False)
    mask_here = lax.dynamic_index_in_dim(mask_rows.reshape(2, 2, 2, 8), col, 3, keepdims=False)
    mask_core = lax.dynamic_index_in_dim(mask_rows, core, 2, keepdims=False)
    first_col = (half + y_lo * 2 + core) % 2 * 8 + col
    row_hit = down[:, :, None] == 8 * jnp.arange(4) + z
    col_hit = over[:, :, None] == 16 * jnp.arange(2) + first_col
    place = (
        row_hit[:, :, None, :, None]
        & col_hit[:, None, :, None, :]
        & (mask_here > 0)[:, :, :, None, None]
    ).astype(F32)
    panel_hit = lax.dynamic_index_in_dim(maps, core, 1, keepdims=False) == core
    panel_place = (row_hit & (mask_core > 0)[:, :, None] & panel_hit[:, None, None]).astype(F32)

    place = jnp.where(half == 1, place[::-1], place)
    special = jnp.where(
        jnp.logical_and(half == 0, col == 0), 0, jnp.where(jnp.logical_and(half == 1, col == 1), 1, 2)
    )
    where = jnp.stack([z, special, core]).astype(jnp.int32)
    spread_y, spread_z = ring_y(y), ring_z(z)
    swap = lambda value: lax.ppermute(value, "y_hi", [(0, 1), (1, 0)])

    lead = jnp.concatenate([parent[:B, :B], child[:B, :B]], axis=0)
    held = spread_y.start(lead)
    from0, from4 = spread_y.end(held)
    base = jnp.where(core == 0, from0[:B], from4[:B]).astype(F32)
    childs = [from0[B:].astype(F32), from4[B:].astype(F32)]
    top = base + panel_place[0, 0, 0] * childs[0] + panel_place[1, 0, 0] * childs[1]
    sibling = swap(tie(child, held))
    rest = jnp.concatenate([parent[B:, :B], child[B:, :B]], axis=0)
    rest_held = spread_y.start(tie(rest, held))
    top_held = spread_z.start(top)
    pivot_rows = jnp.concatenate(spread_z.end(tie(top_held, rest_held)), axis=0)
    theirs = other(tie(pivot_rows, sibling))

    strip = parent[:B].astype(F32).reshape(B, 2, B)
    for k, ref in ((0, child[:B]), (1, sibling[:B])):
        for b in range(2):
            strip += place[k, 0, b, 0][None, :, None] * ref[:, None, b * B : (b + 1) * B].astype(F32)
    strip_held = spread_z.start(tie(strip.reshape(B, 2 * B).astype(BF16), pivot_rows))
    rest0, rest4 = spread_y.end(tie(rest_held, pivot_rows))

    x0, l10, low = first_pivot(where, pivot_rows, theirs)
    g, h = spread_z.end(tie(strip_held, x0))
    tiles = jnp.where(core == 0, rest0[: 3 * B], rest4[: 3 * B]).astype(F32)
    below = [
        tiles[(s - 1) * B : s * B]
        + panel_place[0, s // 3, s] * (rest0[3 * B :].astype(F32) if s == 3 else childs[0])
        + panel_place[1, s // 3, s] * (rest4[3 * B :].astype(F32) if s == 3 else childs[1])
        for s in range(1, 4)
    ]
    column = jnp.concatenate([top, *below], axis=0)
    column_other = other(tie(column, x0))
    x1 = second_pivot(tie(low, column))
    out = finish(
        place.reshape(-1), where, parent, child, sibling, column, column_other,
        g, h, x0, x1, l10,
    )
    return out[None]


def solution(mesh):
    shape = mesh.shape
    if (shape["front"], shape["row"], shape["col"]) != (8, 8, 8):
        raise ValueError("mesh shape")
    fine = Mesh(
        mesh.devices.reshape(4, 2, 8, 4, 2), ("x", "y_hi", "row", "y_lo", "core")
    )
    spec = P(("x", "y_hi"), "row", ("y_lo", "core"))
    return jax.shard_map(
        on_device, mesh=fine, in_specs=(spec, spec, P(), P()), out_specs=spec, check_vma=False
    )
```

```python
import jax
import jax.numpy as jnp
from jax import lax
from jax.experimental import pallas as pl
from jax.experimental.pallas import tpu as pltpu
from jax.sharding import Mesh
from jax.sharding import PartitionSpec as P

B = 256
H = 128
F32 = jnp.float32
BF16 = jnp.bfloat16


def matmul(a, b, dims, precision=lax.Precision.HIGHEST):
    return lax.dot_general(a, b, (dims, ((), ())), precision=precision, preferred_element_type=F32)


NT = ((1,), (1,))
NN = ((1,), (0,))


def split(a):
    high = a.astype(BF16)
    return high, (a - high.astype(F32)).astype(BF16)


def three_pass(a, b, dims):
    (ah, al), (bh, bl) = a, b
    dot = lambda x, y: lax.dot_general(x, y, (dims, ((), ())), preferred_element_type=F32)
    return dot(ah, bh) + (dot(ah, bl) + dot(al, bh))


def inverse_factor(strips):
    sub = lax.broadcasted_iota(jnp.int32, (8, H), 0)
    lane = lax.broadcasted_iota(jnp.int32, (8, H), 1)
    count = H // 8
    body = list(strips)
    inv = [(lane == sub + 8 * s).astype(F32) for s in range(count)]
    row_of = lambda v, j: jnp.broadcast_to(v[j : j + 1, :], (8, H))
    for s in range(count):
        cols = {
            t: [jnp.broadcast_to(body[t][:, 8 * s + j : 8 * s + j + 1], (8, H)) for j in range(8)]
            for t in range(s, count)
        }
        for j in range(8):
            scale = lax.rsqrt(row_of(cols[s][j], j))
            row_body = row_of(body[s], j) * scale
            row_inv = row_of(inv[s], j) * scale
            own = cols[s][j] * scale
            coeff = {m: row_of(own, m) for m in range(j + 1, 8)}
            for t in range(s, count):
                col = own if t == s else cols[t][j] * scale
                for m in range(j + 1, 8):
                    cols[t][m] = cols[t][m] - col * coeff[m]
                if t == s:
                    low = jnp.where(sub > j, col, 0.0)
                    body[t] = body[t] - low * row_body
                    inv[t] = jnp.where(sub == j, row_inv, inv[t] - low * row_inv)
                else:
                    body[t] = body[t] - col * row_body
                    inv[t] = inv[t] - col * row_inv
    return jnp.concatenate(inv, axis=0)


def at(k):
    return slice(k * H, (k + 1) * H)


def factor_tile(work, first):
    inv, low = {}, {}
    last = first + 1
    for b in (first, last):
        inv[b] = inverse_factor(
            [work[b * H + 8 * s : b * H + 8 * s + 8, at(b)] for s in range(H // 8)]
        )
        if b == first:
            low = matmul(work[at(last), at(b)], inv[b], NT)
            work[at(last), at(last)] -= matmul(low, low, NT)
    return inv[first], inv[last], -matmul(inv[last], matmul(low, inv[first], NN), NN)


def store_inverse(x_ref, blocks):
    top, low, corner = blocks
    x_ref[0:H, 0:H] = top
    x_ref[H:, H:] = low
    x_ref[0:H, H:] = jnp.zeros((H, H), F32)
    x_ref[H:, 0:H] = corner


def first_kernel(where, row0_ref, row1_ref, theirs_ref, x0_ref, l10_ref, rest_ref, work):
    even = where[2] == 0
    work[...] = jnp.where(even, row0_ref[...], theirs_ref[...])
    store_inverse(x0_ref, factor_tile(work, 0))
    d10 = jnp.where(even, row1_ref[...], row0_ref[...].T)
    low = matmul(d10, x0_ref[...], NT)
    l10_ref[...] = low
    rest_ref[...] = jnp.where(even, theirs_ref[...], row1_ref[...]) - matmul(low, low, NT)


def second_kernel(rest_ref, x1_ref, work):
    work[...] = rest_ref[...]
    store_inverse(x1_ref, factor_tile(work, 0))


TILE = jax.ShapeDtypeStruct((B, B), F32)
VMEM = pl.BlockSpec(memory_space=pltpu.VMEM)
COST = pl.CostEstimate(flops=10**10, bytes_accessed=2**20, transcendentals=0)
PARAMS = pltpu.CompilerParams(vmem_limit_bytes=32 * 2**20)


def first_pivot(where, row0, row1, theirs):
    return pl.pallas_call(
        first_kernel,
        out_shape=(TILE, TILE, TILE),
        in_specs=[pl.BlockSpec(memory_space=pltpu.SMEM), VMEM, VMEM, VMEM],
        scratch_shapes=[pltpu.VMEM((B, B), F32)],
        compiler_params=PARAMS,
        cost_estimate=COST,
    )(where, row0, row1, theirs)


def second_pivot(rest):
    return pl.pallas_call(
        second_kernel,
        out_shape=TILE,
        in_specs=[VMEM],
        scratch_shapes=[pltpu.VMEM((B, B), F32)],
        compiler_params=PARAMS,
        cost_estimate=COST,
    )(rest)


def final_kernel(
    place, where, parent_ref, own_ref, sib_ref, mine_ref, theirs_ref, g_ref, h_ref,
    x0_ref, x1_ref, l10_ref, out_ref, across, xs,
):
    slot = pl.program_id(0)

    @pl.when(slot == 0)
    def _():
        for k, ref in enumerate((x0_ref, x1_ref, l10_ref)):
            xs[2 * k], xs[2 * k + 1] = split(ref[...])
        x0, x1, l10 = [(xs[2 * k], xs[2 * k + 1]) for k in range(3)]
        dot = lambda a, b: lax.dot_general(a, b, (NN, ((), ())), preferred_element_type=F32)
        g = g_ref[...]
        q0 = dot(x0[0], g) + dot(x0[1], g)
        q1 = three_pass(x1, split(h_ref[...].astype(F32) - three_pass(l10, split(q0), NN)), NN)
        across[0:B] = q0.astype(BF16)
        across[B:] = q1.astype(BF16)

    x0, x1, l10 = [(xs[2 * k], xs[2 * k + 1]) for k in range(3)]
    even = where[2] == 0
    mine, theirs = mine_ref[...], theirs_ref[...]
    p0 = three_pass(split(jnp.where(even, mine, theirs)), x0, NT)
    p0s = split(p0)
    p1 = three_pass(split(jnp.where(even, theirs, mine) - three_pass(p0s, l10, NT)), x1, NT)
    p1s = split(p1)
    row = where[0] + 8 * slot
    lead = row < 2
    last = (slot == 3).astype(jnp.int32)
    from_row = pl.multiple_of(last * B, B)
    for v in range(2):
        cols = slice(v * B, (v + 1) * B)
        value = parent_ref[:, cols].astype(F32)
        for b in range(v + 1):
            here = slice(b * B, (b + 1) * B)
            for child, ref in enumerate((own_ref, sib_ref)):
                part = ref[pl.ds(from_row, B), here].astype(F32)
                w = place[(((child * 2 + last) * 2 + b) * 4 + slot) * 2 + v]
                value += w * part
        q0, q1 = across[0:B, cols], across[B:, cols]
        dot = lambda a, b: lax.dot_general(a, b, (NN, ((), ())), preferred_element_type=F32)
        value -= (dot(p0s[0], q0) + dot(p1s[0], q1)) + (dot(p0s[1], q0) + dot(p1s[1], q1))
        out_ref[:, cols] = jnp.where(lead, 0.0, value)
    tril = lax.broadcasted_iota(jnp.int32, (B, B), 0) >= lax.broadcasted_iota(jnp.int32, (B, B), 1)

    @pl.when(where[1] == 0)
    def _():
        out_ref[:, 0:B] = jnp.where(jnp.logical_or(tril, row > 0), p0, 0.0)

    @pl.when(where[1] == 1)
    def _():
        keep = jnp.logical_and(jnp.logical_or(tril, row > 1), row > 0)
        out_ref[:, 0:B] = jnp.where(keep, p1, 0.0)


def finish(place, where, parent, own, sib, mine, theirs, g, h, x0, x1, l10):
    whole = lambda shape: pl.BlockSpec(shape, lambda i, *_: (0, 0))
    rows = lambda width: pl.BlockSpec((B, width), lambda i, *_: (i, 0))
    wide, tile = whole((B, 2 * B)), whole((B, B))
    return pl.pallas_call(
        final_kernel,
        out_shape=jax.ShapeDtypeStruct(parent.shape, F32),
        grid_spec=pltpu.PrefetchScalarGridSpec(
            num_scalar_prefetch=2,
            grid=(parent.shape[0] // B,),
            in_specs=[
                rows(2 * B), whole((2 * B, 2 * B)), whole((2 * B, 2 * B)), rows(B), rows(B),
                wide, wide, tile, tile, tile,
            ],
            out_specs=rows(2 * B),
            scratch_shapes=[pltpu.VMEM((2 * B, 2 * B), BF16), pltpu.VMEM((6, B, B), BF16)],
        ),
        compiler_params=pltpu.CompilerParams(vmem_limit_bytes=48 * 2**20),
    )(place, where, parent, own, sib, mine, theirs, g, h, x0, x1, l10)


def tie(value, *after):
    return lax.optimization_barrier((value, *after))[0]


def one_of(index, places):
    hit = index == places[0]
    for place in places[1:]:
        hit = jnp.logical_or(hit, index == place)
    return hit


class Along:
    def __init__(self, axes, index, first, second, third, fourth, zero, one):
        self.axes, self.index = axes, index
        self.routes = first, second, third, fourth
        self.zero, self.one = zero, one

    def send(self, value, k):
        return lax.ppermute(value, self.axes, self.routes[k])

    def start(self, block):
        first, second = self.send(block, 0), self.send(block, 1)
        ends = lambda k: [dst for _, dst in self.routes[k]]
        return jnp.where(
            one_of(self.index, ends(0)), first, jnp.where(one_of(self.index, ends(1)), second, block)
        )

    def end(self, held):
        third, fourth = self.send(held, 2), self.send(held, 3)
        pick = lambda own, near: jnp.where(
            one_of(self.index, own), held, jnp.where(one_of(self.index, near), third, fourth)
        )
        return pick(*self.zero), pick(*self.one)


def ring_y(y):
    return Along(
        ("y_hi", "y_lo"), y, [(0, 3), (4, 7)], [(0, 5), (4, 1)],
        [(0, 1), (3, 4), (5, 6), (4, 5), (7, 0), (1, 2)], [(0, 7), (3, 2), (4, 3), (7, 6)],
        ((0, 3, 5), (1, 4, 6)), ((4, 7, 1), (5, 0, 2)),
    )


def ring_z(z):
    return Along(
        "row", z, [(0, 5), (1, 4)], [(0, 2), (1, 7)],
        [(0, 1), (5, 4), (2, 3), (1, 2), (4, 5), (7, 6)], [(0, 7), (5, 6), (1, 0), (4, 3)],
        ((0, 2, 5), (1, 3, 4)), ((1, 4, 7), (2, 5, 6)),
    )


def on_device(parent, child, child_blocks, child_mask):
    parent, child = parent[0], child[0]
    x, half = lax.axis_index("x"), lax.axis_index("y_hi")
    z, y_lo, core = lax.axis_index("row"), lax.axis_index("y_lo"), lax.axis_index("core")
    z = z.astype(jnp.int32)
    y = half * 4 + y_lo
    col = 2 * y_lo + core
    other = lambda value: lax.ppermute(value, "core", [(0, 1), (1, 0)])

    maps = lax.dynamic_slice(child_blocks, (2 * x, 0), (2, 16))
    masks = lax.dynamic_slice(child_mask, (2 * x, 0, 0), (2, 16, 16))
    down = lax.dynamic_index_in_dim(maps.reshape(2, 2, 8), z, 2, keepdims=False)
    over = lax.dynamic_index_in_dim(maps.reshape(2, 2, 8), col, 2, keepdims=False)
    mask_rows = lax.dynamic_index_in_dim(masks.reshape(2, 2, 8, 16), z, 2, keepdims=False)
    mask_here = lax.dynamic_index_in_dim(mask_rows.reshape(2, 2, 2, 8), col, 3, keepdims=False)
    mask_core = lax.dynamic_index_in_dim(mask_rows, core, 2, keepdims=False)
    first_col = (half + y_lo * 2 + core) % 2 * 8 + col
    row_hit = down[:, :, None] == 8 * jnp.arange(4) + z
    col_hit = over[:, :, None] == 16 * jnp.arange(2) + first_col
    place = (
        row_hit[:, :, None, :, None]
        & col_hit[:, None, :, None, :]
        & (mask_here > 0)[:, :, :, None, None]
    ).astype(F32)
    panel_hit = lax.dynamic_index_in_dim(maps, core, 1, keepdims=False) == core
    panel_place = (row_hit & (mask_core > 0)[:, :, None] & panel_hit[:, None, None]).astype(F32)

    place = jnp.where(half == 1, place[::-1], place)
    special = jnp.where(
        jnp.logical_and(half == 0, col == 0), 0, jnp.where(jnp.logical_and(half == 1, col == 1), 1, 2)
    )
    where = jnp.stack([z, special, core]).astype(jnp.int32)
    spread_y, spread_z = ring_y(y), ring_z(z)
    swap = lambda value: lax.ppermute(value, "y_hi", [(0, 1), (1, 0)])

    lead = jnp.concatenate([parent[:B, :B], child[:B, :B]], axis=0)
    held = spread_y.start(lead)
    from0, from4 = spread_y.end(held)
    base = jnp.where(core == 0, from0[:B], from4[:B]).astype(F32)
    childs = [from0[B:].astype(F32), from4[B:].astype(F32)]
    top = base + panel_place[0, 0, 0] * childs[0] + panel_place[1, 0, 0] * childs[1]
    sibling = swap(tie(child, held))
    rest = jnp.concatenate([parent[B:, :B], child[B:, :B]], axis=0)
    rest_held = spread_y.start(tie(rest, held))
    top_held = spread_z.start(top)
    row0, row1 = spread_z.end(tie(top_held, rest_held))
    mine = jnp.where(core == 0, row0, row1)
    theirs = other(mine)

    strip = parent[:B].astype(F32).reshape(B, 2, B)
    for k, ref in ((0, child[:B]), (1, sibling[:B])):
        for b in range(2):
            strip += place[k, 0, b, 0][None, :, None] * ref[:, None, b * B : (b + 1) * B].astype(F32)
    strip_held = spread_z.start(tie(strip.reshape(B, 2 * B).astype(BF16), mine))
    rest0, rest4 = spread_y.end(tie(rest_held, mine))

    x0, l10, low = first_pivot(tie(where, sibling), row0, row1, theirs)
    g, h = spread_z.end(tie(strip_held, x0))
    tiles = jnp.where(core == 0, rest0[: 3 * B], rest4[: 3 * B]).astype(F32)
    below = [
        tiles[(s - 1) * B : s * B]
        + panel_place[0, s // 3, s] * (rest0[3 * B :].astype(F32) if s == 3 else childs[0])
        + panel_place[1, s // 3, s] * (rest4[3 * B :].astype(F32) if s == 3 else childs[1])
        for s in range(1, 4)
    ]
    column = jnp.concatenate([top, *below], axis=0)
    column_other = other(tie(column, x0))
    x1 = second_pivot(tie(low, column))
    out = finish(
        place.reshape(-1), where, parent, child, sibling, column, column_other,
        g, h, x0, x1, l10,
    )
    return out[None]


def solution(mesh):
    shape = mesh.shape
    if (shape["front"], shape["row"], shape["col"]) != (8, 8, 8):
        raise ValueError("mesh shape")
    fine = Mesh(
        mesh.devices.reshape(4, 2, 8, 4, 2), ("x", "y_hi", "row", "y_lo", "core")
    )
    spec = P(("x", "y_hi"), "row", ("y_lo", "core"))
    return jax.shard_map(
        on_device, mesh=fine, in_specs=(spec, spec, P(), P()), out_specs=spec, check_vma=False
    )
```
